32 devices in a mesh: group: 2 (over x), ep: 16 (over z, y, core).
Axes of the slice: x: 2, y: 2, z: 4, core: 2. Of those that a mesh axis runs over, the one named last changes fastest.
Arguments:
- tokens: bfloat16 [2048, 3584], P(('group', 'ep')), parts along dimension 0, may hold values from -6 to 6
- expert_ids: int32 [2048, 4], P(('group', 'ep')), parts along dimension 0, may hold values from 0 to 7, all different within a row; in each aligned block of 64 rows (0 to 63, 64 to 127, ...) at most 36 rows name the same one
- gate_weights: float32 [2048, 4], P(('group', 'ep')), parts along dimension 0, may hold values from 0.1 to 0.5
- w_gate: bfloat16 [3584, 8192], P(None, 'ep'), may hold values from -0.09375 to 0.09375
- w_up: bfloat16 [3584, 8192], P(None, 'ep'), may hold values from -0.09375 to 0.09375
- w_down: bfloat16 [8192, 3584], P('ep'), may hold values from -0.1875 to 0.1875
- prefill_latent: bfloat16 [2048, 576], P(('group', 'ep')), parts along dimension 0, may hold values from -6 to 6
- page_target: int32 [128], P(('group', 'ep')), parts along dimension 0, may hold values from 0 to 15, as said below
- queries: bfloat16 [32, 64, 576], P(('group', 'ep')), parts along dimension 0, may hold values from -400 to 400
- cache_latent: bfloat16 [32, 256, 576], P(('group', 'ep')), parts along dimension 0, may hold values from -7 to 7
- cache_len: int32 [32], P(('group', 'ep')), parts along dimension 0, may hold values from 1 to 256, 2048 in all
Outputs:
- moe_out: bfloat16 [2048, 3584], P(('group', 'ep')), parts along dimension 0
- attn_out: bfloat16 [32, 64, 512], P(('group', 'ep')), parts along dimension 0
The draws below stay inside these ranges and needn't reach their ends.
There are 2 independent parts, one for each index of `group`. The reference program is written for one: setup_inputs(seed, part) draws one part's arguments, and reference() takes and returns one part's arrays. A program takes and returns all parts, laid end to end along the dimension named above; an argument that names none is the same for every part. Nothing has to cross between parts.
Inputs may be any that keep to these rules, and one draw needn't show every extreme that they name: `expert_ids`: each row names 4 different experts; among the rows of one device no expert is named by more than 36 rows. `page_target`: request r belongs to the device with index r // 1 along ep. The pages of one device name requests of pairwise different devices; some request is named by one page of every device. `cache_len`: some request holds exactly 256 positions.
All inputs are finite; a program needn't handle non-finite values. No bound on the sum of `cache_len` on one device may be relied on, other than what follows from the above.
Results may differ from the reference program's by a relative error of at most 0.008.
Values may be sent and summed in bfloat16 or wider, within the bound.
A program may use at most 128 MiB of HBM per device.

```python
import math
import jax
import jax.numpy as jnp
import numpy as np
from jax import lax

D = 3584
FFW = 1024
SPLIT = 2
LAT = 512
ROPE = 64
NH = 64
PAGE = 16
TOK_DEV = 64
DEC_DEV = 1
CACHE = 256
KD = 576
EXPERTS = 8
TOPK = 4
CAP = 36
TOKENS = 1024
REQS = 16
N_EP = 16


def cache_field(key):
    base = jax.random.truncated_normal(key, -6.0, 6.0, (REQS, CACHE, LAT + ROPE), jnp.float32)
    second = base[:, 1, LAT:]
    return base.at[:, 1, LAT:].set(second)


def draw_cache_latent(key, part):
    field = cache_field(key)
    return field.astype(jnp.bfloat16)


def draw_queries(key, part):
    key = jax.random.fold_in(key, 5)
    base = 1.25 * jax.random.truncated_normal(key, -6.0, 6.0, (REQS, NH, LAT + ROPE), jnp.float32)
    return base.astype(jnp.bfloat16)


def draw_page_target(key, part):
    key = jax.random.fold_in(key, 7)
    per_dev = TOK_DEV // PAGE
    hot_owner = jax.random.randint(jax.random.fold_in(key, 1), (), 0, N_EP, dtype=jnp.int32)
    hot_pick = jax.random.randint(jax.random.fold_in(key, 2), (), 0, DEC_DEV, dtype=jnp.int32)

    def one_device(index):
        device_key = jax.random.fold_in(key, 100 + index)
        offsets = jax.random.permutation(device_key, N_EP - 1)[:per_dev - 1].astype(jnp.int32) + 1
        owners = jnp.concatenate([hot_owner[None], (hot_owner + offsets) % N_EP]).astype(jnp.int32)
        picks = jax.random.randint(jax.random.fold_in(device_key, 3), (per_dev,), 0, DEC_DEV, dtype=jnp.int32)
        picks = picks.at[0].set(hot_pick)
        requests = owners * DEC_DEV + picks
        shift = jax.random.randint(jax.random.fold_in(device_key, 4), (), 0, per_dev, dtype=jnp.int32)
        return jnp.roll(requests, shift)
    table = jax.vmap(one_device)(jnp.arange(N_EP, dtype=jnp.int32))
    return table.reshape(-1).astype(jnp.int32)


def block_levels(stream_key, dims, cuts, smallest, top_value):
    level, own = 1.0, jax.random.fold_in(stream_key, 6)
    for position, blocks in cuts:
        draws = jnp.exp(jax.random.uniform(jax.random.fold_in(own, position), (blocks,), jnp.float32, smallest / len(cuts), top_value / len(cuts)))
        level = level * jnp.repeat(draws, dims[position] // blocks).reshape([-1 if axis == position else 1 for axis in range(len(dims))])
    return level


def length_profile(count, total, limit, skew):
    portions = [(1 << 20) // math.isqrt(standing ** skew) + 1 for standing in range(2, count + 1)]
    spare, holding = total - limit - (count - 1), [1] * (count - 1)
    while spare > 0:
        candidates = [i for i in range(count - 1) if holding[i] < limit]
        whole, left = sum([portions[i] for i in candidates]), spare
        for i in candidates:
            extra = min(limit - holding[i], max(1, left * portions[i] // whole), spare)
            holding[i] = holding[i] + extra
            spare = spare - extra
    return np.array([limit] + holding)


def uneven_parts(key, amount, total, reach, lean):
    if amount == 2:
        one = jax.random.randint(key, (), max(1, total - reach), min(reach, total - 1) + 1)
        return jnp.stack([one, total - one])
    sizes = jnp.asarray(length_profile(amount, total, reach, lean), jnp.int32)
    couples = (amount - 1) // 2
    source_of, sink = sizes[1:1 + 2 * couples:2], sizes[2:2 + 2 * couples:2]
    room = jnp.minimum(source_of - 1, reach - sink)
    passed = jax.random.randint(jax.random.fold_in(key, 1), (couples,), 0, 1 << 20) % (room + 1)
    sizes = sizes.at[1:1 + 2 * couples:2].set(source_of - passed).at[2:2 + 2 * couples:2].set(sink + passed)
    return sizes[jax.random.permutation(jax.random.fold_in(key, 2), amount)]


def routed_block(own_key, own, number, rows, amount, top, most, skew):
    order = jax.random.permutation(own_key, amount)
    heavy_load, common = shares(amount, rows * top, most, skew, True), shares(amount, rows * top, most, skew, False)
    places = jnp.arange(amount)

    def named(tallies, offset_by):
        used = int((tallies > 0).sum())
        fixed = max(1, used // 4)
        moved = fixed + (places - fixed + offset_by * (used - fixed)) % max(1, amount - fixed)
        return jnp.zeros((amount,), jnp.int32).at[order[jnp.where(places < fixed, places, moved)]].set(jnp.asarray(tallies, jnp.int32))

    tallies = jnp.where(number % 4 == 0, named(heavy_load, number // 4), named(common, number - number // 4 - 1))
    mixed = jax.random.permutation(jax.random.fold_in(own, 3), amount)
    giver, taker = mixed[0:amount // 2 * 2:2], mixed[1:amount // 2 * 2:2]
    slack = jnp.minimum(tallies[giver] - 1, most - tallies[taker]) // 2
    slack = jnp.where((giver == order[0]) | (taker == order[0]) | (tallies[taker] == 0), 0, jnp.maximum(slack, 0))
    moved = jax.random.randint(jax.random.fold_in(own, 4), (amount // 2,), 0, 1 << 20) % (slack + 1)
    tallies = tallies.at[giver].add(-moved).at[taker].add(moved)
    members = jnp.searchsorted(jnp.cumsum(tallies), jnp.arange(rows * top), side="right").astype(jnp.int32)
    listing = members.reshape(top, rows).T
    listing = listing[jax.random.permutation(jax.random.fold_in(own, 1), rows)]
    offset_by = jax.random.randint(jax.random.fold_in(own, 2), (rows, 1), 0, top)
    return jnp.take_along_axis(listing, (jnp.arange(top)[None, :] + offset_by) % top, axis=1)


def shares(amount, total, limit, slope, full):
    weights = [(1 << 20) // math.isqrt(grade ** slope) + 1 for grade in range(1, amount + 1)]
    largest = limit if full else min(limit, max(-(-total // amount), total * weights[0] // sum(weights)))
    least = 1 if total - largest >= amount - 1 else 0
    holding, spare = [largest] + [least] * (amount - 1), total - largest - least * (amount - 1)
    while spare > 0:
        movable = [i for i in range(1, amount) if holding[i] < largest] or [i for i in range(1, amount) if holding[i] < limit]
        mass, budget = sum([weights[i] for i in movable]), spare
        for i in movable:
            addition = min(limit - holding[i], max(1, budget * weights[i] // mass), spare)
            holding[i] = holding[i] + addition
            spare = spare - addition
    return np.array(holding)


def centred(own_key, shape, spread, most, split=(), kind=jnp.bfloat16):
    values = spread * jax.random.normal(own_key, shape, jnp.float32)
    if split:
        values = values * block_levels(own_key, shape, split, -0.22, 0.18)
    return jnp.clip(values, -most, most).astype(kind)


def setup_inputs(seed: int = 0, part: int = 0) -> dict:
    streams_of = jax.random.split(jax.random.key(seed), 12)
    own_keys = jax.random.split(jax.random.fold_in(streams_of[11], part), 12)
    tokens = centred(own_keys[0], (TOKENS, D), 1.0, 6.0, ((0, 16),))
    expert_ids_keys = jax.random.split(jax.random.fold_in(own_keys[1], 1), TOKENS // TOK_DEV)
    expert_ids_turns = jax.random.permutation(jax.random.fold_in(own_keys[1], 3), TOKENS // TOK_DEV)
    expert_ids = jax.vmap(lambda own, number: routed_block(jax.random.fold_in(own_keys[1], 2), own, number, TOK_DEV, EXPERTS, TOPK, CAP, 2))(expert_ids_keys, expert_ids_turns).reshape((TOKENS, TOPK))
    gate_weights = jnp.clip(0.1 + 0.4 * jax.random.uniform(own_keys[2], (TOKENS, TOPK), jnp.float32) ** block_levels(own_keys[2], (TOKENS, TOPK), ((0, 16),), -0.2, 0.2), 0.1, 0.5)
    w_gate = centred(streams_of[3], (D, EXPERTS * FFW), D ** -0.5, 0.09375, ((1, 16),))
    w_up = centred(streams_of[4], (D, EXPERTS * FFW), D ** -0.5, 0.09375, ((1, 16),))
    w_down = centred(streams_of[5], (EXPERTS * FFW, D), FFW ** -0.5, 0.1875, ((0, 16),))
    prefill_latent = centred(own_keys[6], (TOKENS, KD), 1.0, 6.0, ((0, 16),))
    page_target = draw_page_target(jax.random.fold_in(jax.random.fold_in(streams_of[11], part), 71), part)
    queries = draw_queries(jax.random.fold_in(jax.random.fold_in(streams_of[11], part), 71), part)
    cache_latent = draw_cache_latent(jax.random.fold_in(jax.random.fold_in(streams_of[11], part), 71), part)
    cache_len = uneven_parts(own_keys[10], REQS, REQS * CACHE // 2, CACHE, 2).astype(jnp.int32)
    return {"tokens": tokens, "expert_ids": expert_ids, "gate_weights": gate_weights, "w_gate": w_gate, "w_up": w_up, "w_down": w_down, "prefill_latent": prefill_latent, "page_target": page_target, "queries": queries, "cache_latent": cache_latent, "cache_len": cache_len}


score_scale = 192.0 ** -0.5
mask_low = -1e30


def reference(tokens, expert_ids, gate_weights, w_gate, w_up, w_down, prefill_latent, page_target, queries, cache_latent, cache_len):
    per_block = TOK_DEV * TOPK
    flat = expert_ids.reshape(N_EP, per_block)
    onehot = (flat[:, :, None] == jnp.arange(EXPERTS, dtype=jnp.int32)[None, None, :]).astype(jnp.int32)
    before = jnp.cumsum(onehot, axis=1) - onehot
    slot = jnp.sum(before * onehot, axis=2).astype(jnp.int32)
    dest = (flat * CAP + slot).astype(jnp.int32)
    token_of = (jnp.arange(N_EP, dtype=jnp.int32)[:, None] * TOK_DEV + jnp.arange(per_block, dtype=jnp.int32)[None, :] // TOPK).astype(jnp.int32)
    blocks = jnp.broadcast_to(jnp.arange(N_EP, dtype=jnp.int32)[:, None], (N_EP, per_block))
    table_tok = jnp.zeros((N_EP, EXPERTS * CAP), jnp.int32).at[blocks, dest].set(token_of)
    table_weight = jnp.zeros((N_EP, EXPERTS * CAP), jnp.float32).at[blocks, dest].set(gate_weights.reshape(N_EP, per_block))
    gate_all = w_gate.reshape(D, EXPERTS, FFW)
    up_all = w_up.reshape(D, EXPERTS, FFW)
    down_all = w_down.reshape(EXPERTS, SPLIT, FFW // SPLIT, D)

    def expert_step(result, expert):
        start = (expert * CAP).astype(jnp.int32)
        rows_at = lax.dynamic_slice_in_dim(table_tok, start, CAP, 1).reshape(-1)
        scaling = lax.dynamic_slice_in_dim(table_weight, start, CAP, 1).reshape(-1)
        rows = tokens[rows_at]
        gate = jnp.dot(rows, gate_all[:, expert, :], preferred_element_type=jnp.float32)
        upward = jnp.dot(rows, up_all[:, expert, :], preferred_element_type=jnp.float32)
        hidden = (jax.nn.silu(gate) * upward).astype(jnp.bfloat16)
        pieces = hidden.reshape(-1, SPLIT, FFW // SPLIT).astype(jnp.float32)
        partial_value = jnp.einsum("rsf,sfd->rsd", pieces, down_all[expert].astype(jnp.float32), precision=lax.Precision.HIGHEST)
        output = jnp.sum(partial_value.astype(jnp.bfloat16).astype(jnp.float32), axis=1)
        result = result.at[rows_at].add(scaling[:, None] * output)
        return result, None

    result, _ = lax.scan(expert_step, jnp.zeros((TOKENS, D), jnp.float32), jnp.arange(EXPERTS, dtype=jnp.int32))
    moe_out = result.astype(jnp.bfloat16)

    tok_target = jnp.repeat(page_target, PAGE)

    def one_request(index):
        keys = jnp.concatenate([cache_latent[index], prefill_latent], axis=0)
        valid = jnp.concatenate([jnp.arange(CACHE, dtype=jnp.int32) < cache_len[index], tok_target == index])
        scores = jnp.dot(queries[index], keys.T, preferred_element_type=jnp.float32) * score_scale
        peak = jnp.max(jnp.where(valid[None, :], scores, mask_low), axis=1)
        weight = jnp.where(valid[None, :], jnp.exp(scores - peak[:, None]), 0.0)
        total = jnp.sum(weight, axis=1)
        summed = jnp.dot(weight.astype(jnp.bfloat16), keys[:, :LAT], preferred_element_type=jnp.float32)
        return (summed / total[:, None]).astype(jnp.bfloat16)

    attn_out = lax.map(one_request, jnp.arange(REQS, dtype=jnp.int32))
    return moe_out, attn_out
```

```python
import jax
import jax.numpy as jnp
from jax import lax
from jax.sharding import PartitionSpec as P

SPLIT = 2
LAT = 512
PAGE = 16


score_scale = 192.0 ** (-0.5)
mask_low = -1e30


def experts_part(tokens, expert_ids, gate_weights, w_gate, w_up, w_down):
    owners = lax.axis_size("ep")
    experts = owners // SPLIT
    flat = jnp.sum(
        jnp.where(
            expert_ids[:, :, None] == jnp.arange(experts, dtype=jnp.int32)[None, None, :],
            gate_weights[:, :, None],
            0.0,
        ),
        axis=1,
    )
    rows = lax.all_gather(tokens, "ep", axis=0, tiled=True)
    mixing = lax.all_to_all(
        jnp.repeat(flat.T, SPLIT, axis=0), "ep", split_axis=0, concat_axis=0, tiled=True
    ).reshape(-1)
    gate = jnp.dot(rows, w_gate, preferred_element_type=jnp.float32)
    upward = jnp.dot(rows, w_up, preferred_element_type=jnp.float32)
    hidden = (jax.nn.silu(gate) * upward).astype(jnp.bfloat16)
    done = jnp.dot(hidden, w_down, preferred_element_type=jnp.float32)
    done = (done * mixing[:, None]).astype(jnp.bfloat16)
    return lax.psum_scatter(done, "ep", scatter_dimension=0, tiled=True)


def decode_part(prefill_latent, page_target, queries, cache_latent, cache_len):
    dec_count = queries.shape[0]
    positions = cache_latent.shape[1]
    mine = lax.axis_index("ep") * dec_count + jnp.arange(dec_count, dtype=jnp.int32)
    scores = (
        jnp.einsum("rhk,rck->rhc", queries, cache_latent, preferred_element_type=jnp.float32)
        * score_scale
    )
    valid = (jnp.arange(positions, dtype=jnp.int32)[None, :] < cache_len[:, None])[:, None, :]
    peak = jnp.max(jnp.where(valid, scores, mask_low), axis=2)
    weight = jnp.where(valid, jnp.exp(scores - peak[:, :, None]), 0.0)
    total = jnp.sum(weight, axis=2)
    summed = jnp.einsum(
        "rhc,rcv->rhv",
        weight.astype(jnp.bfloat16),
        cache_latent[:, :, :LAT],
        preferred_element_type=jnp.float32,
    )
    old_summed = summed
    latent_rows = lax.all_gather(prefill_latent, "ep", axis=0, tiled=True)
    page_owner = lax.all_gather(page_target, "ep", axis=0, tiled=True)
    row_target = jnp.repeat(page_owner, PAGE)
    match = (row_target[None, :] == mine[:, None])[:, None, :]
    piece_scores = (
        jnp.einsum("rhk,tk->rht", queries, latent_rows, preferred_element_type=jnp.float32)
        * score_scale
    )
    piece_peak = jnp.max(jnp.where(match, piece_scores, mask_low), axis=2)
    new_peak = jnp.maximum(peak, piece_peak)
    piece_weight = jnp.where(match, jnp.exp(piece_scores - new_peak[:, :, None]), 0.0)
    shrink = jnp.exp(peak - new_peak)
    new_total = total * shrink + jnp.sum(piece_weight, axis=2)
    added = jnp.einsum(
        "rht,tv->rhv",
        piece_weight.astype(jnp.bfloat16),
        latent_rows[:, :LAT],
        preferred_element_type=jnp.float32,
    )
    summed = old_summed * shrink[:, :, None] + added
    return (summed / new_total[:, :, None]).astype(jnp.bfloat16)


def local(tokens, expert_ids, gate_weights, w_gate, w_up, w_down, prefill_latent, page_target, queries, cache_latent, cache_len):
    moe_out = experts_part(tokens, expert_ids, gate_weights, w_gate, w_up, w_down)
    attn_out = decode_part(prefill_latent, page_target, queries, cache_latent, cache_len)
    return (moe_out, attn_out)


def solution(mesh):
    placed = (
        P(("group", "ep"), None),
        P(("group", "ep"), None),
        P(("group", "ep"), None),
        P(None, "ep"),
        P(None, "ep"),
        P("ep", None),
        P(("group", "ep"), None),
        P(("group", "ep")),
        P(("group", "ep"), None, None),
        P(("group", "ep"), None, None),
        P(("group", "ep")),
    )
    return jax.shard_map(
        local,
        mesh=mesh,
        in_specs=placed,
        out_specs=(P(("group", "ep"), None), P(("group", "ep"), None, None)),
        check_vma=False,
    )
```

```python
import jax
import jax.numpy as jnp
from jax import lax
from jax.experimental import pallas as pl
from jax.experimental.pallas import tpu as pltpu
from jax.sharding import PartitionSpec as P

SPLIT = 2
LAT = 512
PAGE = 16


score_scale = 192.0 ** (-0.5)
mask_low = -1e30


def experts_part(tokens, expert_ids, gate_weights, w_gate, w_up, w_down):
    owners = lax.axis_size("ep")
    experts = owners // SPLIT
    flat = jnp.sum(
        jnp.where(
            expert_ids[:, :, None] == jnp.arange(experts, dtype=jnp.int32)[None, None, :],
            gate_weights[:, :, None],
            0.0,
        ),
        axis=1,
    )
    rows = lax.all_gather(tokens, "ep", axis=0, tiled=True)
    mixing = lax.all_to_all(
        jnp.repeat(flat.T, SPLIT, axis=0), "ep", split_axis=0, concat_axis=0, tiled=True
    ).reshape(-1)
    gate = jnp.dot(rows, w_gate, preferred_element_type=jnp.float32)
    upward = jnp.dot(rows, w_up, preferred_element_type=jnp.float32)
    hidden = (jax.nn.silu(gate) * upward).astype(jnp.bfloat16)
    done = jnp.dot(hidden, w_down, preferred_element_type=jnp.float32)
    done = (done * mixing[:, None]).astype(jnp.bfloat16)
    return lax.psum_scatter(done, "ep", scatter_dimension=0, tiled=True)


def decode_part(prefill_latent, page_target, queries, cache_latent, cache_len):
    dec_count = queries.shape[0]
    positions = cache_latent.shape[1]
    mine = lax.axis_index("ep") * dec_count + jnp.arange(dec_count, dtype=jnp.int32)
    scores = (
        jnp.einsum("rhk,rck->rhc", queries, cache_latent, preferred_element_type=jnp.float32)
        * score_scale
    )
    valid = (jnp.arange(positions, dtype=jnp.int32)[None, :] < cache_len[:, None])[:, None, :]
    peak = jnp.max(jnp.where(valid, scores, mask_low), axis=2)
    weight = jnp.where(valid, jnp.exp(scores - peak[:, :, None]), 0.0)
    total = jnp.sum(weight, axis=2)
    summed = jnp.einsum(
        "rhc,rcv->rhv",
        weight.astype(jnp.bfloat16),
        cache_latent[:, :, :LAT],
        preferred_element_type=jnp.float32,
    )
    old_summed = summed
    latent_rows = lax.all_gather(prefill_latent, "ep", axis=0, tiled=True)
    page_owner = lax.all_gather(page_target, "ep", axis=0, tiled=True)
    row_target = jnp.repeat(page_owner, PAGE)
    match = (row_target[None, :] == mine[:, None])[:, None, :]
    piece_scores = (
        jnp.einsum("rhk,tk->rht", queries, latent_rows, preferred_element_type=jnp.float32)
        * score_scale
    )
    piece_peak = jnp.max(jnp.where(match, piece_scores, mask_low), axis=2)
    new_peak = jnp.maximum(peak, piece_peak)
    piece_weight = jnp.where(match, jnp.exp(piece_scores - new_peak[:, :, None]), 0.0)
    shrink = jnp.exp(peak - new_peak)
    new_total = total * shrink + jnp.sum(piece_weight, axis=2)
    added = jnp.einsum(
        "rht,tv->rhv",
        piece_weight.astype(jnp.bfloat16),
        latent_rows[:, :LAT],
        preferred_element_type=jnp.float32,
    )
    summed = old_summed * shrink[:, :, None] + added
    return (summed / new_total[:, :, None]).astype(jnp.bfloat16)


PLANES = 4
CHUNKS = 4
CONTRACT_LAST = (((1,), (1,)), ((), ()))
BF16, F32 = jnp.bfloat16, jnp.float32


def fused_kernel(
    tok_ref, ids_ref, gw_ref, wg_hbm, wu_hbm, wd_hbm, lat_ref, page_ref, q_ref, cache_ref, len_ref,
    moe_ref, attn_ref,
    xg, wg, wu, wd, hid, part, from_sib, to_y, from_y, to_z, from_z,
    w_sem, ag_send, ag_recv, sib_send, sib_recv, y_send, y_recv, z_send, z_recv,
):
    me = lax.axis_index("ep")
    z, y, c = me // 4, (me // 2) % 2, me % 2
    expert = me // 2
    rows, width = tok_ref.shape
    keys = lat_ref.shape[1]
    plane_rows = 4 * rows
    ffw = wg.shape[1]
    cols = width // CHUNKS
    sib = z * 4 + y * 2 + (1 - c)
    across = z * 4 + (1 - y) * 2 + c
    above, below = me + 4, me - 4
    upper = z // 2
    near = z * (1 - upper) + (PLANES - 1 - z) * upper
    is_end = near == 0
    is_inner = near == 1

    def plane_of(s):
        q = jnp.where(s == 0, near, jnp.where(s == 1, 1 - near, s))
        return q * (1 - upper) + (PLANES - 1 - q) * upper

    def row_at(block):
        return pl.ds(pl.multiple_of(block * rows, rows), rows)

    def at_plane(p):
        return pl.ds(pl.multiple_of(p * plane_rows, plane_rows), plane_rows)

    def remote(src, dst, send, recv, to):
        return pltpu.make_async_remote_copy(
            src_ref=src, dst_ref=dst, send_sem=send, recv_sem=recv,
            device_id={"ep": to}, device_id_type=pl.DeviceIdType.MESH,
        )

    def gather_copy(block, route, p, to):
        return remote(xg.at[row_at(block)], xg.at[row_at(block)], ag_send.at[route, p], ag_recv.at[block], to)

    loads = [
        pltpu.make_async_copy(wg_hbm, wg, w_sem.at[0]),
        pltpu.make_async_copy(wu_hbm, wu, w_sem.at[1]),
        pltpu.make_async_copy(wd_hbm, wd, w_sem.at[2]),
    ]
    for load in loads:
        load.start()

    barrier = pltpu.get_barrier_semaphore()
    for to in (sib, across):
        pl.semaphore_signal(barrier, inc=1, device_id={"ep": to}, device_id_type=pl.DeviceIdType.MESH)

    @pl.when(z < PLANES - 1)
    def _():
        pl.semaphore_signal(barrier, inc=1, device_id={"ep": above}, device_id_type=pl.DeviceIdType.MESH)

    @pl.when(z > 0)
    def _():
        pl.semaphore_signal(barrier, inc=1, device_id={"ep": below}, device_id_type=pl.DeviceIdType.MESH)

    own = row_at(me)
    xg[own, 0:width] = tok_ref[...]
    lane = lax.broadcasted_iota(jnp.int32, (rows, 64), 1)
    line = lax.broadcasted_iota(jnp.int32, (rows, 64), 0)
    ids, gw = ids_ref[...], gw_ref[...]
    dense = jnp.zeros((rows, 64), F32)
    for k in range(ids.shape[1]):
        dense = dense + jnp.where(lane % 8 == ids[:, k : k + 1], gw[:, k : k + 1], 0.0)
    high = dense.astype(BF16).astype(F32)
    mid = (dense - high).astype(BF16).astype(F32)
    low = dense - high - mid
    target = jnp.zeros((rows, 64), F32)
    for j in range(rows // PAGE):
        target = target + jnp.where(line // PAGE == j, page_ref[j].astype(F32), 0.0)
    extra = jnp.where(
        lane < 8, high, jnp.where(lane < 16, mid, jnp.where(lane < 24, low, jnp.where(lane == 24, target, 0.0)))
    )
    xg[own, width : width + LAT] = lat_ref[:, :LAT]
    xg[own, width + LAT :] = jnp.concatenate([lat_ref[:, LAT:].astype(F32), extra], axis=1).astype(BF16)

    pl.semaphore_wait(barrier, 3 + jnp.where(is_inner, 1, 0))

    def arrive(s):
        p = plane_of(s)
        block = p * 4 + y * 2 + c
        if s > 0:
            gather_copy(block, 0, p, sib).wait_recv()

        @pl.when((p <= z) & (z < PLANES - 1))
        def _():
            gather_copy(block, 0, p, above).start()

        @pl.when((p >= z) & (z > 0))
        def _():
            gather_copy(block, 1, p, below).start()

        gather_copy(block, 2, p, across).start()
        gather_copy(block, 3, p, sib).start()

    def sib_copy(p, side, ch, core):
        block = p * 4 + side * 2 + core
        at = pl.ds(pl.multiple_of(ch * cols, 128), cols)
        return remote(
            part.at[row_at(block), at], from_sib.at[row_at(p * 2 + side), at],
            sib_send.at[side, p, ch], sib_recv.at[side, p, ch], sib,
        )

    def y_copy(p, ch):
        at = pl.ds(pl.multiple_of(ch * cols, 128), cols)
        return remote(to_y.at[row_at(p), at], from_y.at[row_at(p), at], y_send.at[p, ch], y_recv.at[p, ch], across)

    def z_copy(p, ch, way, to):
        at = pl.ds(pl.multiple_of(ch * cols, 128), cols)
        return remote(
            to_z.at[row_at(p), at], from_z.at[way, row_at(p), at], z_send.at[p, ch], z_recv.at[way, p, ch], to
        )

    def experts_on(p):
        at = at_plane(p)

        @pl.loop(0, ffw // 256)
        def _(f):
            fs = pl.ds(pl.multiple_of(f * 256, 256), 256)
            gate = jnp.dot(xg[at, 0:width], wg[:, fs], preferred_element_type=F32)
            upward = jnp.dot(xg[at, 0:width], wu[:, fs], preferred_element_type=F32)
            hid[:, fs] = (gate / (1.0 + jnp.exp(-gate)) * upward).astype(BF16)

        tile = xg[at, width + LAT :].astype(F32)
        spot = lax.broadcasted_iota(jnp.int32, tile.shape, 1) - 64
        chosen = (spot >= 0) & (spot < 24) & (spot % 8 == expert)
        scale = jnp.sum(jnp.where(chosen, tile, 0.0), axis=1, keepdims=True)

        @pl.loop(0, CHUNKS)
        def _(ch):
            cs = pl.ds(pl.multiple_of(ch * cols, 128), cols)
            out = jnp.dot(hid[...], wd[:, cs], preferred_element_type=F32)
            part[at, cs] = (out * scale).astype(BF16)
            for side in range(2):
                sib_copy(p, side, ch, 1 - c).start()

    def sum_pair(p):
        @pl.loop(0, CHUNKS)
        def _(ch):
            cs = pl.ds(pl.multiple_of(ch * cols, 128), cols)
            sib_copy(p, 0, ch, c).wait_recv()
            sib_copy(p, 1, ch, c).wait_recv()
            mine = part[row_at(p * 4 + (1 - y) * 2 + c), cs].astype(F32)
            to_y[row_at(p), cs] = (mine + from_sib[row_at(p * 2 + (1 - y)), cs].astype(F32)).astype(BF16)
            y_copy(p, ch).start()

    def column_sum(p, cs):
        total = part[row_at(p * 4 + y * 2 + c), cs].astype(F32)
        total = total + from_sib[row_at(p * 2 + y), cs].astype(F32)
        return total + from_y[row_at(p), cs].astype(F32)

    def pass_on(p):
        @pl.loop(0, CHUNKS)
        def _(ch):
            cs = pl.ds(pl.multiple_of(ch * cols, 128), cols)
            y_copy(p, ch).wait_recv()

            @pl.when(is_end)
            def _():
                to_z[row_at(p), cs] = column_sum(p, cs).astype(BF16)

            @pl.when(is_inner)
            def _():
                way = jnp.where(p > z, 0, 1)
                z_copy(p, ch, way, sib).wait_recv()
                to_z[row_at(p), cs] = (column_sum(p, cs) + from_z[way, row_at(p), cs].astype(F32)).astype(BF16)

            @pl.when(p > z)
            def _():
                z_copy(p, ch, 0, above).start()

            @pl.when(p < z)
            def _():
                z_copy(p, ch, 1, below).start()

    def finish():
        @pl.loop(0, CHUNKS)
        def _(ch):
            cs = pl.ds(pl.multiple_of(ch * cols, 128), cols)
            y_copy(z, ch).wait_recv()

            @pl.when(z > 0)
            def _():
                z_copy(z, ch, 0, sib).wait_recv()

            @pl.when(z < PLANES - 1)
            def _():
                z_copy(z, ch, 1, sib).wait_recv()

            total = column_sum(z, cs)

            @pl.when(is_inner)
            def _():
                both = from_z[0, row_at(z), cs].astype(F32) + from_z[1, row_at(z), cs].astype(F32)
                moe_ref[:, cs] = (total + both).astype(BF16)

            @pl.when(is_end)
            def _():
                moe_ref[:, cs] = (total + from_z[1 - upper, row_at(z), cs].astype(F32)).astype(BF16)

    def attend():
        q = q_ref[0]
        cached = lax.dot_general(q, cache_ref[0], CONTRACT_LAST, preferred_element_type=F32) * score_scale
        fresh = lax.dot_general(q, xg[:, width : width + keys], CONTRACT_LAST, preferred_element_type=F32)
        fresh = fresh * score_scale
        pick = (lax.broadcasted_iota(jnp.int32, (8, 128), 1) == 64 + 24).astype(F32).astype(BF16)
        wanted = lax.dot_general(pick, xg[:, width + LAT :], CONTRACT_LAST, preferred_element_type=F32)[0:1, :]
        match = jnp.abs(wanted - me.astype(F32)) < 0.5
        valid = lax.broadcasted_iota(jnp.int32, cached.shape, 1) < len_ref[0]
        peak = jnp.maximum(
            jnp.max(jnp.where(valid, cached, mask_low), axis=1, keepdims=True),
            jnp.max(jnp.where(match, fresh, mask_low), axis=1, keepdims=True),
        )
        w_old = jnp.where(valid, jnp.exp(cached - peak), 0.0)
        w_new = jnp.where(match, jnp.exp(fresh - peak), 0.0)
        total = jnp.sum(w_old, axis=1, keepdims=True) + jnp.sum(w_new, axis=1, keepdims=True)
        summed = jnp.dot(w_old.astype(BF16), cache_ref[0, :, :LAT], preferred_element_type=F32)
        summed = summed + jnp.dot(w_new.astype(BF16), xg[:, width : width + LAT], preferred_element_type=F32)
        attn_ref[0] = (summed / total).astype(BF16)

    arrive(0)

    @pl.loop(0, PLANES)
    def _(s):
        @pl.when(s == 0)
        def _():
            arrive(1)

        @pl.when((is_inner & (s == 0)) | (is_end & (s == 1)))
        def _():
            arrive(2)

        @pl.when((is_inner & (s == 1)) | (is_end & (s == 2)))
        def _():
            arrive(3)

        p = plane_of(s)
        crossed = p * 4 + (1 - y) * 2 + c
        gather_copy(crossed, 0, p, sib).wait_recv()
        gather_copy(crossed, 4, p, sib).start()
        gather_copy(p * 4 + y * 2 + (1 - c), 0, p, sib).wait_recv()
        gather_copy(p * 4 + (1 - y) * 2 + (1 - c), 0, p, sib).wait_recv()

        @pl.when(s == 0)
        def _():
            for load in loads:
                load.wait()

        experts_on(p)
        sum_pair(p)

        @pl.when(is_end & (s == 2))
        def _():
            pass_on(plane_of(1))

    attend()
    pass_on(plane_of(2))
    pass_on(plane_of(3))

    @pl.when(is_inner)
    def _():
        pass_on(plane_of(1))

    finish()

    @pl.loop(0, PLANES)
    def _(p):
        block = p * 4 + y * 2 + c

        @pl.when((p <= z) & (z < PLANES - 1))
        def _():
            gather_copy(block, 0, p, above).wait_send()

        @pl.when((p >= z) & (z > 0))
        def _():
            gather_copy(block, 1, p, below).wait_send()

        gather_copy(block, 2, p, across).wait_send()
        gather_copy(block, 3, p, sib).wait_send()
        gather_copy(p * 4 + (1 - y) * 2 + c, 4, p, sib).wait_send()

        @pl.loop(0, CHUNKS)
        def _(ch):
            for side in range(2):
                sib_copy(p, side, ch, 1 - c).wait_send()
            y_copy(p, ch).wait_send()

            @pl.when(p != z)
            def _():
                z_copy(p, ch, 0, sib).wait_send()


def fused(tokens, expert_ids, gate_weights, w_gate, w_up, w_down, prefill_latent, page_target, queries, cache_latent, cache_len):
    rows, width = tokens.shape
    keys = prefill_latent.shape[1]
    ffw = w_gate.shape[1]
    count = lax.axis_size("ep")
    vmem = pl.BlockSpec(memory_space=pltpu.VMEM)
    smem = pl.BlockSpec(memory_space=pltpu.SMEM)
    hbm = pl.BlockSpec(memory_space=pl.ANY)
    dma = pltpu.SemaphoreType.DMA
    return pl.pallas_call(
        fused_kernel,
        out_shape=(
            jax.ShapeDtypeStruct((rows, width), BF16),
            jax.ShapeDtypeStruct((1, queries.shape[1], LAT), BF16),
        ),
        in_specs=[vmem, vmem, vmem, hbm, hbm, hbm, vmem, smem, vmem, vmem, smem],
        out_specs=(vmem, vmem),
        scratch_shapes=[
            pltpu.VMEM((count * rows, width + keys + 64), BF16),
            pltpu.VMEM((width, ffw), BF16),
            pltpu.VMEM((width, ffw), BF16),
            pltpu.VMEM((ffw, width), BF16),
            pltpu.VMEM((4 * rows, ffw), BF16),
            pltpu.VMEM((count * rows, width), BF16),
            pltpu.VMEM((count // 2 * rows, width), BF16),
            pltpu.VMEM((PLANES * rows, width), BF16),
            pltpu.VMEM((PLANES * rows, width), BF16),
            pltpu.VMEM((PLANES * rows, width), BF16),
            pltpu.VMEM((2, PLANES * rows, width), BF16),
            dma((3,)),
            dma((5, PLANES)),
            dma((count,)),
            dma((2, PLANES, CHUNKS)),
            dma((2, PLANES, CHUNKS)),
            dma((PLANES, CHUNKS)),
            dma((PLANES, CHUNKS)),
            dma((PLANES, CHUNKS)),
            dma((2, PLANES, CHUNKS)),
        ],
        compiler_params=pltpu.CompilerParams(
            collective_id=0, has_side_effects=True, vmem_limit_bytes=60 * 1024 * 1024
        ),
    )(tokens, expert_ids, gate_weights, w_gate, w_up, w_down, prefill_latent, page_target, queries, cache_latent, cache_len)


def local(tokens, expert_ids, gate_weights, w_gate, w_up, w_down, prefill_latent, page_target, queries, cache_latent, cache_len):
    if lax.axis_size("ep") == 16 and queries.shape[0] == 1:
        return fused(
            tokens, expert_ids, gate_weights, w_gate, w_up, w_down,
            prefill_latent, page_target, queries, cache_latent, cache_len,
        )
    moe_out = experts_part(tokens, expert_ids, gate_weights, w_gate, w_up, w_down)
    attn_out = decode_part(prefill_latent, page_target, queries, cache_latent, cache_len)
    return (moe_out, attn_out)


def solution(mesh):
    placed = (
        P(("group", "ep"), None),
        P(("group", "ep"), None),
        P(("group", "ep"), None),
        P(None, "ep"),
        P(None, "ep"),
        P("ep", None),
        P(("group", "ep"), None),
        P(("group", "ep")),
        P(("group", "ep"), None, None),
        P(("group", "ep"), None, None),
        P(("group", "ep")),
    )
    return jax.shard_map(
        local,
        mesh=mesh,
        in_specs=placed,
        out_specs=(P(("group", "ep"), None), P(("group", "ep"), None, None)),
        check_vma=False,
    )
```

```python
import jax
import jax.numpy as jnp
from jax import lax
from jax.experimental import pallas as pl
from jax.experimental.pallas import tpu as pltpu
from jax.sharding import PartitionSpec as P

SPLIT = 2
LAT = 512
PAGE = 16


score_scale = 192.0 ** (-0.5)
mask_low = -1e30


def experts_part(tokens, expert_ids, gate_weights, w_gate, w_up, w_down):
    owners = lax.axis_size("ep")
    experts = owners // SPLIT
    flat = jnp.sum(
        jnp.where(
            expert_ids[:, :, None] == jnp.arange(experts, dtype=jnp.int32)[None, None, :],
            gate_weights[:, :, None],
            0.0,
        ),
        axis=1,
    )
    rows = lax.all_gather(tokens, "ep", axis=0, tiled=True)
    mixing = lax.all_to_all(
        jnp.repeat(flat.T, SPLIT, axis=0), "ep", split_axis=0, concat_axis=0, tiled=True
    ).reshape(-1)
    gate = jnp.dot(rows, w_gate, preferred_element_type=jnp.float32)
    upward = jnp.dot(rows, w_up, preferred_element_type=jnp.float32)
    hidden = (jax.nn.silu(gate) * upward).astype(jnp.bfloat16)
    done = jnp.dot(hidden, w_down, preferred_element_type=jnp.float32)
    done = (done * mixing[:, None]).astype(jnp.bfloat16)
    return lax.psum_scatter(done, "ep", scatter_dimension=0, tiled=True)


def decode_part(prefill_latent, page_target, queries, cache_latent, cache_len):
    dec_count = queries.shape[0]
    positions = cache_latent.shape[1]
    mine = lax.axis_index("ep") * dec_count + jnp.arange(dec_count, dtype=jnp.int32)
    scores = (
        jnp.einsum("rhk,rck->rhc", queries, cache_latent, preferred_element_type=jnp.float32)
        * score_scale
    )
    valid = (jnp.arange(positions, dtype=jnp.int32)[None, :] < cache_len[:, None])[:, None, :]
    peak = jnp.max(jnp.where(valid, scores, mask_low), axis=2)
    weight = jnp.where(valid, jnp.exp(scores - peak[:, :, None]), 0.0)
    total = jnp.sum(weight, axis=2)
    summed = jnp.einsum(
        "rhc,rcv->rhv",
        weight.astype(jnp.bfloat16),
        cache_latent[:, :, :LAT],
        preferred_element_type=jnp.float32,
    )
    old_summed = summed
    latent_rows = lax.all_gather(prefill_latent, "ep", axis=0, tiled=True)
    page_owner = lax.all_gather(page_target, "ep", axis=0, tiled=True)
    row_target = jnp.repeat(page_owner, PAGE)
    match = (row_target[None, :] == mine[:, None])[:, None, :]
    piece_scores = (
        jnp.einsum("rhk,tk->rht", queries, latent_rows, preferred_element_type=jnp.float32)
        * score_scale
    )
    piece_peak = jnp.max(jnp.where(match, piece_scores, mask_low), axis=2)
    new_peak = jnp.maximum(peak, piece_peak)
    piece_weight = jnp.where(match, jnp.exp(piece_scores - new_peak[:, :, None]), 0.0)
    shrink = jnp.exp(peak - new_peak)
    new_total = total * shrink + jnp.sum(piece_weight, axis=2)
    added = jnp.einsum(
        "rht,tv->rhv",
        piece_weight.astype(jnp.bfloat16),
        latent_rows[:, :LAT],
        preferred_element_type=jnp.float32,
    )
    summed = old_summed * shrink[:, :, None] + added
    return (summed / new_total[:, :, None]).astype(jnp.bfloat16)


PLANES = 4
CHUNKS = 4
CONTRACT_LAST = (((1,), (1,)), ((), ()))
BF16, F32 = jnp.bfloat16, jnp.float32


def fused_kernel(
    tok_ref, ids_ref, gw_ref, wg_hbm, wu_hbm, wd_hbm, lat_ref, page_ref, q_ref, cache_ref, len_ref,
    moe_ref, attn_ref,
    xg, wg, wu, wd, hid, part, from_sib, to_y, from_y, to_z, from_z, from_x,
    w_sem, ag_send, ag_recv, sib_send, sib_recv, y_send, y_recv, z_send, z_recv, x_recv,
):
    me = lax.axis_index("ep")
    z, y, c = me // 4, (me // 2) % 2, me % 2
    expert = me // 2
    rows, width = tok_ref.shape
    keys = lat_ref.shape[1]
    plane_rows = 4 * rows
    ffw = wg.shape[1]
    cols = width // CHUNKS
    sib = z * 4 + y * 2 + (1 - c)
    across = z * 4 + (1 - y) * 2 + c
    above, below = me + 4, me - 4
    upper = z // 2
    near = z * (1 - upper) + (PLANES - 1 - z) * upper
    is_end = near == 0
    is_inner = near == 1
    outward = me + 4 - 8 * upper
    inward = me - 4 + 8 * upper

    def plane_of(s):
        q = jnp.where(s == 0, near, jnp.where(s == 1, 1 - near, s))
        return q * (1 - upper) + (PLANES - 1 - q) * upper

    def row_at(block):
        return pl.ds(pl.multiple_of(block * rows, rows), rows)

    def at_plane(p):
        return pl.ds(pl.multiple_of(p * plane_rows, plane_rows), plane_rows)

    def remote(src, dst, send, recv, to):
        return pltpu.make_async_remote_copy(
            src_ref=src, dst_ref=dst, send_sem=send, recv_sem=recv,
            device_id={"ep": to}, device_id_type=pl.DeviceIdType.MESH,
        )

    def gather_copy(block, route, p, to):
        return remote(xg.at[row_at(block)], xg.at[row_at(block)], ag_send.at[route, p], ag_recv.at[block], to)

    loads = [
        pltpu.make_async_copy(wg_hbm, wg, w_sem.at[0]),
        pltpu.make_async_copy(wu_hbm, wu, w_sem.at[1]),
        pltpu.make_async_copy(wd_hbm, wd, w_sem.at[2]),
    ]
    for load in loads:
        load.start()

    barrier = pltpu.get_barrier_semaphore()
    for to in (sib, across):
        pl.semaphore_signal(barrier, inc=1, device_id={"ep": to}, device_id_type=pl.DeviceIdType.MESH)

    @pl.when(z < PLANES - 1)
    def _():
        pl.semaphore_signal(barrier, inc=1, device_id={"ep": above}, device_id_type=pl.DeviceIdType.MESH)

    @pl.when(z > 0)
    def _():
        pl.semaphore_signal(barrier, inc=1, device_id={"ep": below}, device_id_type=pl.DeviceIdType.MESH)

    own = row_at(me)
    xg[own, 0:width] = tok_ref[...]
    lane = lax.broadcasted_iota(jnp.int32, (64, rows), 1)
    line = lax.broadcasted_iota(jnp.int32, (64, rows), 0)
    ids, gw = ids_ref[...], gw_ref[...]
    dense = jnp.zeros((64, rows), F32)
    for k in range(ids.shape[0]):
        dense = dense + jnp.where(line % 8 == ids[k : k + 1, :], gw[k : k + 1, :], 0.0)
    high = dense.astype(BF16).astype(F32)
    mid = (dense - high).astype(BF16).astype(F32)
    low = dense - high - mid
    target = jnp.zeros((64, rows), F32)
    for j in range(rows // PAGE):
        target = target + jnp.where(lane // PAGE == j, page_ref[j].astype(F32), 0.0)
    extra = jnp.where(
        line < 8, high, jnp.where(line < 16, mid, jnp.where(line < 24, low, jnp.where(line == 24, target, 0.0)))
    )
    eye_lane = lax.broadcasted_iota(jnp.int32, (rows, rows), 1)
    eye_line = lax.broadcasted_iota(jnp.int32, (rows, rows), 0)
    eye = (eye_lane == eye_line).astype(F32).astype(BF16)
    extra = lax.dot_general(eye, extra.astype(BF16), CONTRACT_LAST, preferred_element_type=F32)
    xg[own, width : width + LAT] = lat_ref[:, :LAT]
    xg[own, width + LAT :] = jnp.concatenate([lat_ref[:, LAT:].astype(F32), extra], axis=1).astype(BF16)

    pl.semaphore_wait(barrier, 3 + jnp.where(is_inner, 1, 0))

    def arrive(s):
        p = plane_of(s)
        block = p * 4 + y * 2 + c
        if s > 0:
            gather_copy(block, 0, p, sib).wait_recv()

        @pl.when((p <= z) & (z < PLANES - 1))
        def _():
            gather_copy(block, 0, p, above).start()

        @pl.when((p >= z) & (z > 0))
        def _():
            gather_copy(block, 1, p, below).start()

        if s < PLANES - 1:
            gather_copy(block, 2, p, across).start()
        gather_copy(block, 3, p, sib).start()

    def sib_copy(p, side, ch, core):
        block = p * 4 + side * 2 + core
        at = pl.ds(pl.multiple_of(ch * cols, 128), cols)
        return remote(
            part.at[row_at(block), at], from_sib.at[row_at(p * 2 + side), at],
            sib_send.at[side, p, ch], sib_recv.at[side, p, ch], sib,
        )

    def y_copy(p, ch):
        at = pl.ds(pl.multiple_of(ch * cols, 128), cols)
        return remote(to_y.at[row_at(p), at], from_y.at[row_at(p), at], y_send.at[p, ch], y_recv.at[p, ch], across)

    def x_copy(p, ch, slot):
        at = pl.ds(pl.multiple_of(ch * cols, 128), cols)
        return remote(
            to_y.at[row_at(p), at], from_x.at[row_at(slot), at], y_send.at[p, ch], x_recv.at[slot, ch], outward
        )

    def z_copy(p, ch, way, to):
        at = pl.ds(pl.multiple_of(ch * cols, 128), cols)
        return remote(
            to_z.at[row_at(p), at], from_z.at[way, row_at(p), at], z_send.at[p, ch], z_recv.at[way, p, ch], to
        )

    def experts_on(p):
        at = at_plane(p)

        @pl.loop(0, ffw // 256)
        def _(f):
            fs = pl.ds(pl.multiple_of(f * 256, 256), 256)
            gate = jnp.dot(xg[at, 0:width], wg[:, fs], preferred_element_type=F32)
            upward = jnp.dot(xg[at, 0:width], wu[:, fs], preferred_element_type=F32)
            hid[:, fs] = (gate / (1.0 + jnp.exp(-gate)) * upward).astype(BF16)

        tile = xg[at, width + LAT :].astype(F32)
        spot = lax.broadcasted_iota(jnp.int32, tile.shape, 1) - 64
        chosen = (spot >= 0) & (spot < 24) & (spot % 8 == expert)
        scale = jnp.sum(jnp.where(chosen, tile, 0.0), axis=1, keepdims=True)

        @pl.loop(0, CHUNKS)
        def _(ch):
            cs = pl.ds(pl.multiple_of(ch * cols, 128), cols)
            out = jnp.dot(hid[...], wd[:, cs], preferred_element_type=F32)
            part[at, cs] = (out * scale).astype(BF16)
            for side in range(2):
                sib_copy(p, side, ch, 1 - c).start()

    def each_chunk(body):
        @pl.loop(0, CHUNKS)
        def _(ch):
            body(ch, pl.ds(pl.multiple_of(ch * cols, 128), cols))

    def pair_in(p, ch):
        sib_copy(p, 0, ch, c).wait_recv()
        sib_copy(p, 1, ch, c).wait_recv()

    def other_sum(p, cs):
        mine = part[row_at(p * 4 + (1 - y) * 2 + c), cs].astype(F32)
        return mine + from_sib[row_at(p * 2 + (1 - y)), cs].astype(F32)

    def own_sum(p, cs):
        mine = part[row_at(p * 4 + y * 2 + c), cs].astype(F32)
        return mine + from_sib[row_at(p * 2 + y), cs].astype(F32)

    def column_sum(p, cs):
        return own_sum(p, cs) + from_y[row_at(p), cs].astype(F32)

    def send_z(p, ch):
        @pl.when(p > z)
        def _():
            z_copy(p, ch, 0, above).start()

        @pl.when(p < z)
        def _():
            z_copy(p, ch, 1, below).start()

    def cross(p):
        def body(ch, cs):
            pair_in(p, ch)
            to_y[row_at(p), cs] = other_sum(p, cs).astype(BF16)
            y_copy(p, ch).start()

        each_chunk(body)

    def cross_with_far(p):
        def body(ch, cs):
            pair_in(p, ch)
            x_copy(p, ch, 1).wait_recv()
            to_y[row_at(p), cs] = (other_sum(p, cs) + from_x[row_at(1), cs].astype(F32)).astype(BF16)
            y_copy(p, ch).start()

        each_chunk(body)

    def far_first(p):
        def body(ch, cs):
            pair_in(p, ch)
            to_y[row_at(p), cs] = other_sum(p, cs).astype(BF16)
            x_copy(p, ch, 0).start()
            to_z[row_at(p), cs] = own_sum(p, cs).astype(BF16)
            send_z(p, ch)

        each_chunk(body)

    def far_second(p):
        def body(ch, cs):
            pair_in(p, ch)
            x_copy(p, ch, 0).wait_recv()
            to_y[row_at(p), cs] = (other_sum(p, cs) + from_x[row_at(0), cs].astype(F32)).astype(BF16)
            x_copy(p, ch, 1).start()
            way = jnp.where(p > z, 0, 1)
            z_copy(p, ch, way, sib).wait_recv()
            to_z[row_at(p), cs] = (own_sum(p, cs) + from_z[way, row_at(p), cs].astype(F32)).astype(BF16)
            send_z(p, ch)

        each_chunk(body)

    def pass_on(p, chained):
        def body(ch, cs):
            y_copy(p, ch).wait_recv()
            if chained:
                way = jnp.where(p > z, 0, 1)
                z_copy(p, ch, way, sib).wait_recv()
                to_z[row_at(p), cs] = (column_sum(p, cs) + from_z[way, row_at(p), cs].astype(F32)).astype(BF16)
            else:
                to_z[row_at(p), cs] = column_sum(p, cs).astype(BF16)
            send_z(p, ch)

        each_chunk(body)

    def finish():
        @pl.loop(0, CHUNKS)
        def _(ch):
            cs = pl.ds(pl.multiple_of(ch * cols, 128), cols)
            y_copy(z, ch).wait_recv()

            @pl.when(z > 0)
            def _():
                z_copy(z, ch, 0, sib).wait_recv()

            @pl.when(z < PLANES - 1)
            def _():
                z_copy(z, ch, 1, sib).wait_recv()

            total = column_sum(z, cs)

            @pl.when(is_inner)
            def _():
                both = from_z[0, row_at(z), cs].astype(F32) + from_z[1, row_at(z), cs].astype(F32)
                moe_ref[:, cs] = (total + both).astype(BF16)

            @pl.when(is_end)
            def _():
                moe_ref[:, cs] = (total + from_z[1 - upper, row_at(z), cs].astype(F32)).astype(BF16)

    def attend():
        q = q_ref[0]
        cached = jnp.dot(q, cache_ref[0], preferred_element_type=F32) * score_scale
        fresh = lax.dot_general(q, xg[:, width : width + keys], CONTRACT_LAST, preferred_element_type=F32)
        fresh = fresh * score_scale
        pick = (lax.broadcasted_iota(jnp.int32, (8, 128), 1) == 64 + 24).astype(F32).astype(BF16)
        wanted = lax.dot_general(pick, xg[:, width + LAT :], CONTRACT_LAST, preferred_element_type=F32)[0:1, :]
        match = jnp.abs(wanted - me.astype(F32)) < 0.5
        valid = lax.broadcasted_iota(jnp.int32, cached.shape, 1) < len_ref[0]
        peak = jnp.maximum(
            jnp.max(jnp.where(valid, cached, mask_low), axis=1, keepdims=True),
            jnp.max(jnp.where(match, fresh, mask_low), axis=1, keepdims=True),
        )
        w_old = jnp.where(valid, jnp.exp(cached - peak), 0.0)
        w_new = jnp.where(match, jnp.exp(fresh - peak), 0.0)
        total = jnp.sum(w_old, axis=1, keepdims=True) + jnp.sum(w_new, axis=1, keepdims=True)
        summed = lax.dot_general(w_old.astype(BF16), cache_ref[0, :LAT, :], CONTRACT_LAST, preferred_element_type=F32)
        summed = summed + jnp.dot(w_new.astype(BF16), xg[:, width : width + LAT], preferred_element_type=F32)
        attn_ref[0] = (summed / total).astype(BF16)

    arrive(0)

    @pl.loop(0, PLANES)
    def _(s):
        @pl.when(s == 0)
        def _():
            arrive(1)

        @pl.when((is_inner & (s == 0)) | (is_end & (s == 1)))
        def _():
            arrive(2)

        @pl.when((is_inner & (s == 1)) | (is_end & (s == 2)))
        def _():
            arrive(3)

        @pl.when(is_end & (s == 3))
        def _():
            pass_on(plane_of(2), False)

        p = plane_of(s)
        crossed = p * 4 + (1 - y) * 2 + c
        gather_copy(crossed, 0, p, sib).wait_recv()
        gather_copy(crossed, 4, p, sib).start()

        @pl.when(is_inner & (s == 1))
        def _():
            gather_copy(crossed, 5, p, outward).start()

        @pl.when(is_inner & (s == 3))
        def _():
            gather_copy(crossed, 5, p, inward).start()

        gather_copy(p * 4 + y * 2 + (1 - c), 0, p, sib).wait_recv()
        gather_copy(p * 4 + (1 - y) * 2 + (1 - c), 0, p, sib).wait_recv()

        @pl.when(s == 0)
        def _():
            for load in loads:
                load.wait()

        experts_on(p)

        @pl.when((s == 0) | (s == 2) | (is_end & (s == 1)))
        def _():
            cross(p)

        @pl.when(is_end & (s == 2))
        def _():
            pass_on(plane_of(1), False)

        @pl.when(is_end & (s == 3))
        def _():
            far_first(p)

    attend()

    @pl.when(is_inner)
    def _():
        far_second(plane_of(3))
        pass_on(plane_of(2), True)
        cross_with_far(plane_of(1))
        pass_on(plane_of(1), True)

    finish()

    @pl.loop(0, PLANES)
    def _(p):
        block = p * 4 + y * 2 + c

        @pl.when((p <= z) & (z < PLANES - 1))
        def _():
            gather_copy(block, 0, p, above).wait_send()

        @pl.when((p >= z) & (z > 0))
        def _():
            gather_copy(block, 1, p, below).wait_send()

        @pl.when(p != plane_of(3))
        def _():
            gather_copy(block, 2, p, across).wait_send()

        @pl.when(is_inner & ((p == plane_of(1)) | (p == plane_of(3))))
        def _():
            gather_copy(p * 4 + (1 - y) * 2 + c, 5, p, sib).wait_send()

        gather_copy(block, 3, p, sib).wait_send()
        gather_copy(p * 4 + (1 - y) * 2 + c, 4, p, sib).wait_send()

        @pl.loop(0, CHUNKS)
        def _(ch):
            for side in range(2):
                sib_copy(p, side, ch, 1 - c).wait_send()
            y_copy(p, ch).wait_send()

            @pl.when(p != z)
            def _():
                z_copy(p, ch, 0, sib).wait_send()


def fused(tokens, expert_ids, gate_weights, w_gate, w_up, w_down, prefill_latent, page_target, queries, cache_latent, cache_len):
    rows, width = tokens.shape
    keys = prefill_latent.shape[1]
    ffw = w_gate.shape[1]
    count = lax.axis_size("ep")
    vmem = pl.BlockSpec(memory_space=pltpu.VMEM)
    smem = pl.BlockSpec(memory_space=pltpu.SMEM)
    hbm = pl.BlockSpec(memory_space=pl.ANY)
    dma = pltpu.SemaphoreType.DMA
    return pl.pallas_call(
        fused_kernel,
        out_shape=(
            jax.ShapeDtypeStruct((rows, width), BF16),
            jax.ShapeDtypeStruct((1, queries.shape[1], LAT), BF16),
        ),
        in_specs=[vmem, vmem, vmem, hbm, hbm, hbm, vmem, smem, vmem, vmem, smem],
        out_specs=(vmem, vmem),
        scratch_shapes=[
            pltpu.VMEM((count * rows, width + keys + 64), BF16),
            pltpu.VMEM((width, ffw), BF16),
            pltpu.VMEM((width, ffw), BF16),
            pltpu.VMEM((ffw, width), BF16),
            pltpu.VMEM((4 * rows, ffw), BF16),
            pltpu.VMEM((count * rows, width), BF16),
            pltpu.VMEM((count // 2 * rows, width), BF16),
            pltpu.VMEM((PLANES * rows, width), BF16),
            pltpu.VMEM((PLANES * rows, width), BF16),
            pltpu.VMEM((PLANES * rows, width), BF16),
            pltpu.VMEM((2, PLANES * rows, width), BF16),
            pltpu.VMEM((2 * rows, width), BF16),
            dma((3,)),
            dma((6, PLANES)),
            dma((count,)),
            dma((2, PLANES, CHUNKS)),
            dma((2, PLANES, CHUNKS)),
            dma((PLANES, CHUNKS)),
            dma((PLANES, CHUNKS)),
            dma((PLANES, CHUNKS)),
            dma((2, PLANES, CHUNKS)),
            dma((2, CHUNKS)),
        ],
        compiler_params=pltpu.CompilerParams(
            collective_id=0, has_side_effects=True, vmem_limit_bytes=60 * 1024 * 1024
        ),
    )(
        tokens, expert_ids.T, gate_weights.T, w_gate, w_up, w_down, prefill_latent, page_target,
        queries, jnp.swapaxes(cache_latent, 1, 2), cache_len,
    )


def local(tokens, expert_ids, gate_weights, w_gate, w_up, w_down, prefill_latent, page_target, queries, cache_latent, cache_len):
    if lax.axis_size("ep") == 16 and queries.shape[0] == 1:
        return fused(
            tokens, expert_ids, gate_weights, w_gate, w_up, w_down,
            prefill_latent, page_target, queries, cache_latent, cache_len,
        )
    moe_out = experts_part(tokens, expert_ids, gate_weights, w_gate, w_up, w_down)
    attn_out = decode_part(prefill_latent, page_target, queries, cache_latent, cache_len)
    return (moe_out, attn_out)


def solution(mesh):
    placed = (
        P(("group", "ep"), None),
        P(("group", "ep"), None),
        P(("group", "ep"), None),
        P(None, "ep"),
        P(None, "ep"),
        P("ep", None),
        P(("group", "ep"), None),
        P(("group", "ep")),
        P(("group", "ep"), None, None),
        P(("group", "ep"), None, None),
        P(("group", "ep")),
    )
    return jax.shard_map(
        local,
        mesh=mesh,
        in_specs=placed,
        out_specs=(P(("group", "ep"), None), P(("group", "ep"), None, None)),
        check_vma=False,
    )
```

```python
import jax
import jax.numpy as jnp
from jax import lax
from jax.experimental import pallas as pl
from jax.experimental.pallas import tpu as pltpu
from jax.sharding import PartitionSpec as P

SPLIT = 2
LAT = 512
PAGE = 16


score_scale = 192.0 ** (-0.5)
mask_low = -1e30


def experts_part(tokens, expert_ids, gate_weights, w_gate, w_up, w_down):
    owners = lax.axis_size("ep")
    experts = owners // SPLIT
    flat = jnp.sum(
        jnp.where(
            expert_ids[:, :, None] == jnp.arange(experts, dtype=jnp.int32)[None, None, :],
            gate_weights[:, :, None],
            0.0,
        ),
        axis=1,
    )
    rows = lax.all_gather(tokens, "ep", axis=0, tiled=True)
    mixing = lax.all_to_all(
        jnp.repeat(flat.T, SPLIT, axis=0), "ep", split_axis=0, concat_axis=0, tiled=True
    ).reshape(-1)
    gate = jnp.dot(rows, w_gate, preferred_element_type=jnp.float32)
    upward = jnp.dot(rows, w_up, preferred_element_type=jnp.float32)
    hidden = (jax.nn.silu(gate) * upward).astype(jnp.bfloat16)
    done = jnp.dot(hidden, w_down, preferred_element_type=jnp.float32)
    done = (done * mixing[:, None]).astype(jnp.bfloat16)
    return lax.psum_scatter(done, "ep", scatter_dimension=0, tiled=True)


def decode_part(prefill_latent, page_target, queries, cache_latent, cache_len):
    dec_count = queries.shape[0]
    positions = cache_latent.shape[1]
    mine = lax.axis_index("ep") * dec_count + jnp.arange(dec_count, dtype=jnp.int32)
    scores = (
        jnp.einsum("rhk,rck->rhc", queries, cache_latent, preferred_element_type=jnp.float32)
        * score_scale
    )
    valid = (jnp.arange(positions, dtype=jnp.int32)[None, :] < cache_len[:, None])[:, None, :]
    peak = jnp.max(jnp.where(valid, scores, mask_low), axis=2)
    weight = jnp.where(valid, jnp.exp(scores - peak[:, :, None]), 0.0)
    total = jnp.sum(weight, axis=2)
    summed = jnp.einsum(
        "rhc,rcv->rhv",
        weight.astype(jnp.bfloat16),
        cache_latent[:, :, :LAT],
        preferred_element_type=jnp.float32,
    )
    old_summed = summed
    latent_rows = lax.all_gather(prefill_latent, "ep", axis=0, tiled=True)
    page_owner = lax.all_gather(page_target, "ep", axis=0, tiled=True)
    row_target = jnp.repeat(page_owner, PAGE)
    match = (row_target[None, :] == mine[:, None])[:, None, :]
    piece_scores = (
        jnp.einsum("rhk,tk->rht", queries, latent_rows, preferred_element_type=jnp.float32)
        * score_scale
    )
    piece_peak = jnp.max(jnp.where(match, piece_scores, mask_low), axis=2)
    new_peak = jnp.maximum(peak, piece_peak)
    piece_weight = jnp.where(match, jnp.exp(piece_scores - new_peak[:, :, None]), 0.0)
    shrink = jnp.exp(peak - new_peak)
    new_total = total * shrink + jnp.sum(piece_weight, axis=2)
    added = jnp.einsum(
        "rht,tv->rhv",
        piece_weight.astype(jnp.bfloat16),
        latent_rows[:, :LAT],
        preferred_element_type=jnp.float32,
    )
    summed = old_summed * shrink[:, :, None] + added
    return (summed / new_total[:, :, None]).astype(jnp.bfloat16)


PLANES = 4
CHUNKS = 4
CONTRACT_LAST = (((1,), (1,)), ((), ()))
BF16, F32 = jnp.bfloat16, jnp.float32


def fused_kernel(
    tok_ref, ids_ref, gw_ref, wg_hbm, wu_hbm, wd_hbm, lat_ref, page_ref, q_ref, cache_ref, len_ref,
    moe_ref, attn_ref,
    xg, wg, wu, wd, hid, part, from_sib, to_y, from_y, to_z, from_z,
    w_sem, ag_send, ag_recv, sib_send, sib_recv, y_send, y_recv, z_send, z_recv,
):
    me = lax.axis_index("ep")
    z, y, c = me // 4, (me // 2) % 2, me % 2
    expert = me // 2
    rows, width = tok_ref.shape
    keys = lat_ref.shape[1]
    plane_rows = 4 * rows
    ffw = wg.shape[1]
    cols = width // CHUNKS
    sib = z * 4 + y * 2 + (1 - c)
    across = z * 4 + (1 - y) * 2 + c
    above, below = me + 4, me - 4
    upper = z // 2
    near = z * (1 - upper) + (PLANES - 1 - z) * upper
    is_end = near == 0
    is_inner = near == 1
    outward = me + 4 - 8 * upper
    inward = me - 4 + 8 * upper

    def plane_of(s):
        q = jnp.where(s == 0, near, jnp.where(s == 1, 1 - near, s))
        return q * (1 - upper) + (PLANES - 1 - q) * upper

    def row_at(block):
        return pl.ds(pl.multiple_of(block * rows, rows), rows)

    def at_plane(p):
        return pl.ds(pl.multiple_of(p * plane_rows, plane_rows), plane_rows)

    def remote(src, dst, send, recv, to):
        return pltpu.make_async_remote_copy(
            src_ref=src, dst_ref=dst, send_sem=send, recv_sem=recv,
            device_id={"ep": to}, device_id_type=pl.DeviceIdType.MESH,
        )

    def gather_copy(block, route, p, to):
        return remote(xg.at[row_at(block)], xg.at[row_at(block)], ag_send.at[route, p], ag_recv.at[block], to)

    loads = [
        pltpu.make_async_copy(wg_hbm, wg, w_sem.at[0]),
        pltpu.make_async_copy(wu_hbm, wu, w_sem.at[1]),
        pltpu.make_async_copy(wd_hbm, wd, w_sem.at[2]),
    ]
    for load in loads:
        load.start()

    barrier = pltpu.get_barrier_semaphore()
    for to in (sib, across):
        pl.semaphore_signal(barrier, inc=1, device_id={"ep": to}, device_id_type=pl.DeviceIdType.MESH)

    @pl.when(z < PLANES - 1)
    def _():
        pl.semaphore_signal(barrier, inc=1, device_id={"ep": above}, device_id_type=pl.DeviceIdType.MESH)

    @pl.when(z > 0)
    def _():
        pl.semaphore_signal(barrier, inc=1, device_id={"ep": below}, device_id_type=pl.DeviceIdType.MESH)

    own = row_at(me)
    xg[own, 0:width] = tok_ref[...]
    lane = lax.broadcasted_iota(jnp.int32, (64, rows), 1)
    line = lax.broadcasted_iota(jnp.int32, (64, rows), 0)
    ids, gw = ids_ref[...], gw_ref[...]
    dense = jnp.zeros((64, rows), F32)
    for k in range(ids.shape[0]):
        dense = dense + jnp.where(line % 8 == ids[k : k + 1, :], gw[k : k + 1, :], 0.0)
    high = dense.astype(BF16).astype(F32)
    mid = (dense - high).astype(BF16).astype(F32)
    low = dense - high - mid
    target = jnp.zeros((64, rows), F32)
    for j in range(rows // PAGE):
        target = target + jnp.where(lane // PAGE == j, page_ref[j].astype(F32), 0.0)
    extra = jnp.where(
        line < 8, high, jnp.where(line < 16, mid, jnp.where(line < 24, low, jnp.where(line == 24, target, 0.0)))
    )
    eye_lane = lax.broadcasted_iota(jnp.int32, (rows, rows), 1)
    eye_line = lax.broadcasted_iota(jnp.int32, (rows, rows), 0)
    eye = (eye_lane == eye_line).astype(F32).astype(BF16)
    extra = lax.dot_general(eye, extra.astype(BF16), CONTRACT_LAST, preferred_element_type=F32)
    xg[own, width : width + LAT] = lat_ref[:, :LAT]
    xg[own, width + LAT :] = jnp.concatenate([lat_ref[:, LAT:].astype(F32), extra], axis=1).astype(BF16)

    pl.semaphore_wait(barrier, 3 + jnp.where(is_inner, 1, 0))

    def arrive(s):
        p = plane_of(s)
        block = p * 4 + y * 2 + c
        if s > 0:
            gather_copy(block, 0, p, sib).wait_recv()

        @pl.when((p <= z) & (z < PLANES - 1))
        def _():
            gather_copy(block, 0, p, above).start()

        @pl.when((p >= z) & (z > 0))
        def _():
            gather_copy(block, 1, p, below).start()

        if s < PLANES - 1:
            gather_copy(block, 2, p, across).start()
        gather_copy(block, 3, p, sib).start()

    def sib_copy(p, side, ch, core):
        block = p * 4 + side * 2 + core
        at = pl.ds(pl.multiple_of(ch * cols, 128), cols)
        return remote(
            part.at[row_at(block), at], from_sib.at[row_at(p * 2 + side), at],
            sib_send.at[side, p, ch], sib_recv.at[side, p, ch], sib,
        )

    def y_copy(p, ch):
        at = pl.ds(pl.multiple_of(ch * cols, 128), cols)
        return remote(to_y.at[row_at(p), at], from_y.at[row_at(p), at], y_send.at[p, ch], y_recv.at[p, ch], across)

    def z_copy(p, ch, way, to):
        at = pl.ds(pl.multiple_of(ch * cols, 128), cols)
        return remote(
            to_z.at[row_at(p), at], from_z.at[way, row_at(p), at], z_send.at[p, ch], z_recv.at[way, p, ch], to
        )

    def experts_on(p):
        at = at_plane(p)

        @pl.loop(0, ffw // 256)
        def _(f):
            fs = pl.ds(pl.multiple_of(f * 256, 256), 256)
            gate = jnp.dot(xg[at, 0:width], wg[:, fs], preferred_element_type=F32)
            upward = jnp.dot(xg[at, 0:width], wu[:, fs], preferred_element_type=F32)
            hid[:, fs] = (gate / (1.0 + jnp.exp(-gate)) * upward).astype(BF16)

        tile = xg[at, width + LAT :].astype(F32)
        spot = lax.broadcasted_iota(jnp.int32, tile.shape, 1) - 64
        chosen = (spot >= 0) & (spot < 24) & (spot % 8 == expert)
        scale = jnp.sum(jnp.where(chosen, tile, 0.0), axis=1, keepdims=True)

        @pl.loop(0, CHUNKS)
        def _(ch):
            cs = pl.ds(pl.multiple_of(ch * cols, 128), cols)
            out = jnp.dot(hid[...], wd[:, cs], preferred_element_type=F32)
            part[at, cs] = (out * scale).astype(BF16)
            for side in range(2):
                sib_copy(p, side, ch, 1 - c).start()

    def each_chunk(body):
        @pl.loop(0, CHUNKS)
        def _(ch):
            body(ch, pl.ds(pl.multiple_of(ch * cols, 128), cols))

    def pair_in(p, ch):
        sib_copy(p, 0, ch, c).wait_recv()
        sib_copy(p, 1, ch, c).wait_recv()

    def other_sum(p, cs):
        mine = part[row_at(p * 4 + (1 - y) * 2 + c), cs].astype(F32)
        return mine + from_sib[row_at(p * 2 + (1 - y)), cs].astype(F32)

    def own_sum(p, cs):
        mine = part[row_at(p * 4 + y * 2 + c), cs].astype(F32)
        return mine + from_sib[row_at(p * 2 + y), cs].astype(F32)

    def column_sum(p, cs):
        return own_sum(p, cs) + from_y[row_at(p), cs].astype(F32)

    def send_z(p, ch):
        @pl.when(p > z)
        def _():
            z_copy(p, ch, 0, above).start()

        @pl.when(p < z)
        def _():
            z_copy(p, ch, 1, below).start()

    def cross(p):
        def body(ch, cs):
            pair_in(p, ch)
            to_y[row_at(p), cs] = other_sum(p, cs).astype(BF16)
            y_copy(p, ch).start()

        each_chunk(body)

    def pass_on(p, chained):
        def body(ch, cs):
            y_copy(p, ch).wait_recv()
            if chained:
                way = jnp.where(p > z, 0, 1)
                z_copy(p, ch, way, sib).wait_recv()
                to_z[row_at(p), cs] = (column_sum(p, cs) + from_z[way, row_at(p), cs].astype(F32)).astype(BF16)
            else:
                to_z[row_at(p), cs] = column_sum(p, cs).astype(BF16)
            send_z(p, ch)

        each_chunk(body)

    def finish():
        @pl.loop(0, CHUNKS)
        def _(ch):
            cs = pl.ds(pl.multiple_of(ch * cols, 128), cols)
            y_copy(z, ch).wait_recv()

            @pl.when(z > 0)
            def _():
                z_copy(z, ch, 0, sib).wait_recv()

            @pl.when(z < PLANES - 1)
            def _():
                z_copy(z, ch, 1, sib).wait_recv()

            total = column_sum(z, cs)

            @pl.when(is_inner)
            def _():
                both = from_z[0, row_at(z), cs].astype(F32) + from_z[1, row_at(z), cs].astype(F32)
                moe_ref[:, cs] = (total + both).astype(BF16)

            @pl.when(is_end)
            def _():
                moe_ref[:, cs] = (total + from_z[1 - upper, row_at(z), cs].astype(F32)).astype(BF16)

    def attend():
        q = q_ref[0]
        cached = jnp.dot(q, cache_ref[0], preferred_element_type=F32) * score_scale
        fresh = lax.dot_general(q, xg[:, width : width + keys], CONTRACT_LAST, preferred_element_type=F32)
        fresh = fresh * score_scale
        pick = (lax.broadcasted_iota(jnp.int32, (8, 128), 1) == 64 + 24).astype(F32).astype(BF16)
        wanted = lax.dot_general(pick, xg[:, width + LAT :], CONTRACT_LAST, preferred_element_type=F32)[0:1, :]
        match = jnp.abs(wanted - me.astype(F32)) < 0.5
        valid = lax.broadcasted_iota(jnp.int32, cached.shape, 1) < len_ref[0]
        peak = jnp.maximum(
            jnp.max(jnp.where(valid, cached, mask_low), axis=1, keepdims=True),
            jnp.max(jnp.where(match, fresh, mask_low), axis=1, keepdims=True),
        )
        w_old = jnp.where(valid, jnp.exp(cached - peak), 0.0)
        w_new = jnp.where(match, jnp.exp(fresh - peak), 0.0)
        total = jnp.sum(w_old, axis=1, keepdims=True) + jnp.sum(w_new, axis=1, keepdims=True)
        summed = lax.dot_general(w_old.astype(BF16), cache_ref[0, :LAT, :], CONTRACT_LAST, preferred_element_type=F32)
        summed = summed + jnp.dot(w_new.astype(BF16), xg[:, width : width + LAT], preferred_element_type=F32)
        attn_ref[0] = (summed / total).astype(BF16)

    arrive(0)

    @pl.loop(0, PLANES)
    def _(s):
        @pl.when(s == 0)
        def _():
            arrive(1)

        @pl.when((is_inner & (s == 0)) | (is_end & (s == 1)))
        def _():
            arrive(2)

        @pl.when((is_inner & (s == 1)) | (is_end & (s == 2)))
        def _():
            arrive(3)

        @pl.when(is_end & (s == 3))
        def _():
            pass_on(plane_of(2), False)

        p = plane_of(s)
        crossed = p * 4 + (1 - y) * 2 + c
        gather_copy(crossed, 0, p, sib).wait_recv()
        gather_copy(crossed, 4, p, sib).start()

        @pl.when(is_inner & (s == 1))
        def _():
            gather_copy(crossed, 5, p, outward).start()

        @pl.when(is_inner & (s == 3))
        def _():
            gather_copy(crossed, 5, p, inward).start()

        gather_copy(p * 4 + y * 2 + (1 - c), 0, p, sib).wait_recv()
        gather_copy(p * 4 + (1 - y) * 2 + (1 - c), 0, p, sib).wait_recv()

        @pl.when(s == 0)
        def _():
            for load in loads:
                load.wait()

        experts_on(p)

        cross(p)

        @pl.when(is_end & (s == 2))
        def _():
            pass_on(plane_of(1), False)

    attend()

    @pl.when(is_end)
    def _():
        pass_on(plane_of(3), False)

    @pl.when(is_inner)
    def _():
        pass_on(plane_of(2), True)
        pass_on(plane_of(3), True)
        pass_on(plane_of(1), True)

    finish()

    @pl.loop(0, PLANES)
    def _(p):
        block = p * 4 + y * 2 + c

        @pl.when((p <= z) & (z < PLANES - 1))
        def _():
            gather_copy(block, 0, p, above).wait_send()

        @pl.when((p >= z) & (z > 0))
        def _():
            gather_copy(block, 1, p, below).wait_send()

        @pl.when(p != plane_of(3))
        def _():
            gather_copy(block, 2, p, across).wait_send()

        @pl.when(is_inner & ((p == plane_of(1)) | (p == plane_of(3))))
        def _():
            gather_copy(p * 4 + (1 - y) * 2 + c, 5, p, sib).wait_send()

        gather_copy(block, 3, p, sib).wait_send()
        gather_copy(p * 4 + (1 - y) * 2 + c, 4, p, sib).wait_send()

        @pl.loop(0, CHUNKS)
        def _(ch):
            for side in range(2):
                sib_copy(p, side, ch, 1 - c).wait_send()
            y_copy(p, ch).wait_send()

            @pl.when(p != z)
            def _():
                z_copy(p, ch, 0, sib).wait_send()


def fused(tokens, expert_ids, gate_weights, w_gate, w_up, w_down, prefill_latent, page_target, queries, cache_latent, cache_len):
    rows, width = tokens.shape
    keys = prefill_latent.shape[1]
    ffw = w_gate.shape[1]
    count = lax.axis_size("ep")
    vmem = pl.BlockSpec(memory_space=pltpu.VMEM)
    smem = pl.BlockSpec(memory_space=pltpu.SMEM)
    hbm = pl.BlockSpec(memory_space=pl.ANY)
    dma = pltpu.SemaphoreType.DMA
    return pl.pallas_call(
        fused_kernel,
        out_shape=(
            jax.ShapeDtypeStruct((rows, width), BF16),
            jax.ShapeDtypeStruct((1, queries.shape[1], LAT), BF16),
        ),
        in_specs=[vmem, vmem, vmem, hbm, hbm, hbm, vmem, smem, vmem, vmem, smem],
        out_specs=(vmem, vmem),
        scratch_shapes=[
            pltpu.VMEM((count * rows, width + keys + 64), BF16),
            pltpu.VMEM((width, ffw), BF16),
            pltpu.VMEM((width, ffw), BF16),
            pltpu.VMEM((ffw, width), BF16),
            pltpu.VMEM((4 * rows, ffw), BF16),
            pltpu.VMEM((count * rows, width), BF16),
            pltpu.VMEM((count // 2 * rows, width), BF16),
            pltpu.VMEM((PLANES * rows, width), BF16),
            pltpu.VMEM((PLANES * rows, width), BF16),
            pltpu.VMEM((PLANES * rows, width), BF16),
            pltpu.VMEM((2, PLANES * rows, width), BF16),
            dma((3,)),
            dma((6, PLANES)),
            dma((count,)),
            dma((2, PLANES, CHUNKS)),
            dma((2, PLANES, CHUNKS)),
            dma((PLANES, CHUNKS)),
            dma((PLANES, CHUNKS)),
            dma((PLANES, CHUNKS)),
            dma((2, PLANES, CHUNKS)),
        ],
        compiler_params=pltpu.CompilerParams(
            collective_id=0, has_side_effects=True, vmem_limit_bytes=60 * 1024 * 1024
        ),
    )(
        tokens, expert_ids.T, gate_weights.T, w_gate, w_up, w_down, prefill_latent, page_target,
        queries, jnp.swapaxes(cache_latent, 1, 2), cache_len,
    )


def local(tokens, expert_ids, gate_weights, w_gate, w_up, w_down, prefill_latent, page_target, queries, cache_latent, cache_len):
    if lax.axis_size("ep") == 16 and queries.shape[0] == 1:
        return fused(
            tokens, expert_ids, gate_weights, w_gate, w_up, w_down,
            prefill_latent, page_target, queries, cache_latent, cache_len,
        )
    moe_out = experts_part(tokens, expert_ids, gate_weights, w_gate, w_up, w_down)
    attn_out = decode_part(prefill_latent, page_target, queries, cache_latent, cache_len)
    return (moe_out, attn_out)


def solution(mesh):
    placed = (
        P(("group", "ep"), None),
        P(("group", "ep"), None),
        P(("group", "ep"), None),
        P(None, "ep"),
        P(None, "ep"),
        P("ep", None),
        P(("group", "ep"), None),
        P(("group", "ep")),
        P(("group", "ep"), None, None),
        P(("group", "ep"), None, None),
        P(("group", "ep")),
    )
    return jax.shard_map(
        local,
        mesh=mesh,
        in_specs=placed,
        out_specs=(P(("group", "ep"), None), P(("group", "ep"), None, None)),
        check_vma=False,
    )
```
